32 devices in a mesh: outer: 2 (over x), rep: 2 (over core), seq: 8 (over z, y).
Axes of the slice: x: 2, y: 2, z: 4, core: 2. Of those that a mesh axis runs over, the one named last changes fastest.
Arguments:
- tokens: bfloat16 [8, 1536, 8192], P(('outer', 'rep'), 'seq'), parts along dimension 0, may hold values from -6 to 6
- value_weight: bfloat16 [8192, 1024], P('seq'), may hold values from -0.0625 to 0.0625
- value_bias: bfloat16 [1024], replicated, may hold values from -3 to 3
- down_matrices: bfloat16 [32, 8192, 64], P(('outer', 'rep', 'seq')), parts along dimension 0, may hold values from -0.0625 to 0.0625
- up_matrices: bfloat16 [32, 64, 1024], P(('outer', 'rep', 'seq')), parts along dimension 0, may hold values from -0.75 to 0.75
- adapter_of_block: int32 [8], P('outer'), parts along dimension 0, may hold values from 0 to 15
- residency: int32 [32], P('outer'), parts along dimension 0, may hold values from 0 to 15, each once
- block_length: int32 [8], P('outer'), parts along dimension 0, may hold values from 384 to 1536, as said below
Outputs:
- values: bfloat16 [8, 1536, 1024], P(('outer', 'rep'), 'seq'), parts along dimension 0
The draws below stay inside these ranges and needn't reach their ends.
There are 2 independent parts, one for each index of `outer`. The reference program is written for one: setup_inputs(seed, part) draws one part's arguments, and reference() takes and returns one part's arrays. A program takes and returns all parts, laid end to end along the dimension named above; an argument that names none is the same for every part. Nothing has to cross between parts.
Inputs may be any that keep to these rules, and one draw needn't show every extreme that they name: `residency`: every adapter id has its own bank slot. `block_length`: some block of every part is full.
All inputs are finite; a program needn't handle non-finite values.
Results may differ from the reference program's by a relative error of at most 0.0038.
Values may be sent and summed in bfloat16 or wider, within the bound.
A program may use at most 128 MiB of HBM per device.

```python
import math
import jax
import jax.numpy as jnp
import numpy as np
from jax import lax

MODEL_DIM = 8192
VALUE_WIDTH = 1024
LOW_RANK_SIZE = 64
BLOCK = 1536
BLOCKS = 4
ADAPTER_COUNT = 16


def draw_block_length(key, part):
    key = jax.random.fold_in(key, 7)
    key_length, key_full = jax.random.split(key)
    length_draw = jax.random.randint(key_length, (BLOCKS,), BLOCK // 4, BLOCK + 1)
    full_block = jax.random.randint(key_full, (), 0, BLOCKS)
    return jnp.where(jnp.arange(BLOCKS) == full_block, BLOCK, length_draw).astype(jnp.int32)


def set_ends(values, own_key, smallest, high):
    longest = values.shape.index(max(values.shape))
    spots = []
    for shift in (0, 1):
        where = [jax.random.randint(jax.random.fold_in(own_key, axis), (), 0, length) for axis, length in enumerate(values.shape)]
        where[longest] = (where[longest] + shift) % values.shape[longest]
        spots.append(tuple(where))
    return values.at[spots[0]].set(smallest).at[spots[1]].set(high)


def shard_levels(key, extent, pieces, low, high):
    def one(position, blocks):
        heights = jax.random.uniform(jax.random.fold_in(jax.random.fold_in(key, 6), position), (blocks,), jnp.float32, low / len(pieces), high / len(pieces))
        return jnp.repeat(jnp.exp(heights), extent[position] // blocks).reshape((-1,) + (1,) * (len(extent) - position - 1))

    level = one(*pieces[0])
    for cut in pieces[1:]:
        level = level * one(*cut)
    return level


def rank_table(count, lean):
    weights = [(1 << 20) // math.isqrt(grade ** lean) + 1 for grade in range(1, count + 1)]
    scale = 1 + sum(weights) // (1 << 30)
    return np.cumsum(np.array([max(1, weight // scale) for weight in weights]))


def ranked_ids(rng, shape, number_of, skew):
    grid = rank_table(number_of, skew)
    pick = jax.random.randint(jax.random.fold_in(rng, 1), shape, 0, int(grid[number_of - 1]))
    rank = jnp.searchsorted(jnp.asarray(grid, jnp.int32), pick, side="right")
    return jax.random.permutation(jax.random.fold_in(rng, 2), number_of)[rank].astype(jnp.int32)


def gaussian(own_key, dims, width, bound, cuts=(), held_as=jnp.bfloat16):
    drawn = width * jax.random.normal(own_key, dims, jnp.float32)
    if cuts:
        drawn = drawn * shard_levels(own_key, dims, cuts, -0.22, 0.18)
    return jnp.clip(drawn, -bound, bound).astype(held_as)


def setup_inputs(seed: int = 0, part: int = 0) -> dict:
    key_list = jax.random.split(jax.random.key(seed), 9)
    own_keys = jax.random.split(jax.random.fold_in(key_list[8], part), 9)
    tokens = gaussian(own_keys[0], (BLOCKS, BLOCK, MODEL_DIM), 1.0, 6.0, ((0, 2), (1, 8)))
    value_weight = gaussian(key_list[1], (MODEL_DIM, VALUE_WIDTH), MODEL_DIM ** -0.5, 0.0625, ((0, 8),))
    value_bias = gaussian(key_list[2], (VALUE_WIDTH,), 0.5, 3.0)
    down_matrices = gaussian(own_keys[3], (ADAPTER_COUNT, MODEL_DIM, LOW_RANK_SIZE), MODEL_DIM ** -0.5, 0.0625, ((0, 16),))
    up_matrices = gaussian(own_keys[4], (ADAPTER_COUNT, LOW_RANK_SIZE, VALUE_WIDTH), LOW_RANK_SIZE ** -0.5, 0.75, ((0, 16),))
    adapter_of_block = set_ends(ranked_ids(own_keys[5], (BLOCKS,), ADAPTER_COUNT, 2), jax.random.fold_in(own_keys[5], 3), 0, ADAPTER_COUNT - 1).astype(jnp.int32)
    residency = jax.random.permutation(own_keys[6], ADAPTER_COUNT).astype(jnp.int32)
    block_length = draw_block_length(jax.random.fold_in(jax.random.fold_in(key_list[8], part), 71), part)
    return {"tokens": tokens, "value_weight": value_weight, "value_bias": value_bias, "down_matrices": down_matrices, "up_matrices": up_matrices, "adapter_of_block": adapter_of_block, "residency": residency, "block_length": block_length}


def reference(tokens, value_weight, value_bias, down_matrices, up_matrices, adapter_of_block, residency, block_length):
    bank_slot = residency[adapter_of_block]
    positions = jnp.arange(BLOCK, dtype=jnp.int32)
    bias_wide = value_bias.astype(jnp.float32)[None, :]

    def one_block(block_number):
        tokens_of_block = tokens[block_number]
        slot_number = bank_slot[block_number]
        base = jnp.dot(tokens_of_block, value_weight, preferred_element_type=jnp.float32) + bias_wide
        shrunk_rows = jnp.dot(tokens_of_block, down_matrices[slot_number], preferred_element_type=jnp.float32).astype(jnp.bfloat16)
        adapter_update = jnp.dot(shrunk_rows, up_matrices[slot_number], preferred_element_type=jnp.float32)
        live = positions < block_length[block_number]
        return jnp.where(live[:, None], base + adapter_update, 0.0).astype(jnp.bfloat16)

    return lax.map(one_block, jnp.arange(BLOCKS, dtype=jnp.int32))
```

```python
import functools
import jax
import jax.numpy as jnp
from jax import lax
from jax.experimental import pallas as pl
from jax.experimental.pallas import tpu as pltpu
from jax.sharding import PartitionSpec as P

MESH = pl.DeviceIdType.MESH


def grid_of(n):
    near = 1
    while near * near * 4 <= n:
        near *= 2
    return n // near, near


def gather_kernel(
    n, A, B, pick_ref, home_ref, w_ref, bank_ref, w_out, ad_out,
    bank_in, mine, lent, borrowed,
    w_send, w_recv, ad_send, ad_recv, swap_send, swap_recv, lend_sems, local_sems,
):
    o, r, s = lax.axis_index("outer"), lax.axis_index("rep"), lax.axis_index("seq")
    a, b = s // B, s % B
    own, other, sib_own, sib_other = o * 2 + r, (1 - o) * 2 + r, o * 2 + 1 - r, (1 - o) * 2 + 1 - r
    side = {"outer": 1 - o}
    sibling = {"rep": 1 - r}

    barrier = pltpu.get_barrier_semaphore()
    for k in range(1, n):
        pl.semaphore_signal(barrier, inc=1, device_id={"seq": (s + k) % n}, device_id_type=MESH)
    pl.semaphore_signal(barrier, inc=1, device_id=side, device_id_type=MESH)
    pl.semaphore_signal(barrier, inc=1, device_id=sibling, device_id_type=MESH)
    pl.semaphore_wait(barrier, n + 1)

    sent = []

    def start(ok, copy):
        def go():
            copy.start()

        if ok is None:
            go()
        else:
            pl.when(ok)(go)
        sent.append((ok, copy))

    def remote(src, dst, send, recv, device):
        return pltpu.make_async_remote_copy(
            src_ref=src, dst_ref=dst, send_sem=send, recv_sem=recv, device_id=device, device_id_type=MESH
        )

    def both(x, y):
        return x if y is None else (y if x is None else jnp.logical_and(x, y))

    def far(step):
        at = a + step
        ok = jnp.logical_and(at >= 0, at < A)
        return ok, jnp.clip(at, 0, A - 1)

    def near(step):
        at = b + step
        ok = jnp.logical_and(at >= 0, at < B)
        return ok, jnp.clip(at, 0, B - 1)

    class Flow:
        def __init__(self, out, send, recv, wide):
            self.out, self.send, self.recv, self.wide = out, send, recv, wide

        def put(self, ok, src, shard, lane, device):
            start(ok, remote(src, self.out(shard), self.send.at[lane, shard], self.recv(shard), device))

        def far_put(self, ok, src, shard, step):
            there, row = far(step)
            self.put(both(ok, there), src, shard, 0 if step < 0 else 1, {"seq": row * B + b})

        def near_put(self, ok, src, shard, step):
            there, col = near(step)
            self.put(both(ok, there), src, shard, 2 if step < 0 else 3, {"seq": a * B + col})

        def arrive(self, ok, shard):
            block = self.out(shard)

            @pl.when(ok)
            def _():
                pltpu.make_async_copy(block, block, self.recv(shard)).wait()

            return block

        def widen(self, ok, src, shard):
            if self.wide:
                self.put(ok, src, shard, 4, side)
                self.put(ok, src, shard, 5, sibling)

        def begin(self, src):
            for step in (-1, 1):
                self.far_put(None, src, s, step)
            for step in (-1, 1):
                self.near_put(None, src, s, step)

        def wave(self, d):
            rows = []
            for sign in (-1, 1) if d else (1,):
                ok, row = far(sign * d)
                rows.append((ok if d else None, row))
                if d:
                    shard = row * B + b
                    src = self.arrive(ok, shard)
                    self.far_put(ok, src, shard, -sign)
                    for step in (-1, 1):
                        self.near_put(ok, src, shard, step)
                    self.widen(ok, src, shard)
            for row_ok, row in rows:
                for e in range(1, B):
                    for sign in (-1, 1):
                        there, col = near(sign * e)
                        ok = both(row_ok, there)
                        shard = row * B + col
                        src = self.arrive(ok, shard)
                        if e < B - 1:
                            self.near_put(ok, src, shard, -sign)
                        self.widen(ok, src, shard)

        def shards(self, d):
            found = []
            for sign in (-1, 1) if d else (1,):
                row_ok, row = far(sign * d)
                if d:
                    found.append((row_ok, row * B + b))
                for e in range(1, B):
                    for near_sign in (-1, 1):
                        there, col = near(near_sign * e)
                        found.append((both(row_ok if d else None, there), row * B + col))
            return found

    weights = Flow(lambda k: w_out.at[k, own], w_send, lambda k: w_recv.at[own, k], True)
    adapters = Flow(lambda k: ad_out.at[k], ad_send, lambda k: ad_recv.at[k], False)

    def cross(d):
        for ok, shard in weights.shards(d):
            block = w_out.at[shard, other]

            @pl.when(ok)
            def _(block=block, shard=shard):
                pltpu.make_async_copy(block, block, w_recv.at[other, shard]).wait()

            start(ok, remote(block, block, w_send.at[6, shard], w_recv.at[other, shard], sibling))

    for k in range(1, n):
        to = (s + k) % n
        start(None, remote(bank_ref.at[to], bank_in.at[s], swap_send.at[k], swap_recv.at[s], {"seq": to}))
    weights.begin(w_ref.at[own])
    kept = pltpu.make_async_copy(bank_ref.at[s], bank_in.at[s], local_sems.at[0])
    kept.start()
    whole = pltpu.make_async_copy(w_ref, w_out.at[s], local_sems.at[1])
    whole.start()

    weights.wave(0)
    if A > 1:
        weights.wave(1)

    kept.wait()
    for k in range(1, n):
        sender = (s + k) % n
        part = bank_in.at[sender]
        pltpu.make_async_copy(part, part, swap_recv.at[sender]).wait()
    pair = mine.shape[0]
    for c in range(pair):
        lent[c] = bank_in[pick_ref[(1 - r) * pair + c]]
    lend = remote(lent, borrowed, lend_sems.at[0], lend_sems.at[1], sibling)
    lend.start()
    lend.wait()
    for c in range(pair):
        here = home_ref[r * pair + c] == r
        mine[c] = jnp.where(here, bank_in[pick_ref[r * pair + c]], borrowed[c])
    adapters.begin(mine)
    stored = pltpu.make_async_copy(mine, ad_out.at[s], local_sems.at[2])
    stored.start()

    cross(0)
    for d in range(2, A):
        weights.wave(d)
        adapters.wave(d - 2)
        cross(d - 1)
    for d in range(max(A - 2, 0), A):
        adapters.wave(d)
    if A > 1:
        cross(A - 1)
    for k in range(1, n):
        shard = (s + k) % n
        for quarter in (sib_own, sib_other):
            block = w_out.at[shard, quarter]
            pltpu.make_async_copy(block, block, w_recv.at[quarter, shard]).wait()
    whole.wait()
    stored.wait()
    for ok, copy in sent:
        if ok is None:
            copy.wait_send()
        else:
            pl.when(ok)(copy.wait_send)


def gather_all(n, weight, bank, pick, home, pair):
    A, B = grid_of(n)
    quarter_rows, width = weight.shape[0] // 4, weight.shape[1]
    part = bank.shape[1:]
    any_space = pl.BlockSpec(memory_space=pl.ANY)
    scalars = pl.BlockSpec(memory_space=pltpu.SMEM)
    dma = pltpu.SemaphoreType.DMA
    return pl.pallas_call(
        functools.partial(gather_kernel, n, A, B),
        out_shape=(
            jax.ShapeDtypeStruct((n, 4, quarter_rows, width), weight.dtype),
            jax.ShapeDtypeStruct((n, pair) + part, bank.dtype),
        ),
        in_specs=[scalars, scalars, any_space, any_space],
        out_specs=(any_space, any_space),
        scratch_shapes=[
            pltpu.VMEM((n,) + part, bank.dtype),
            pltpu.VMEM((pair,) + part, bank.dtype),
            pltpu.VMEM((pair,) + part, bank.dtype),
            pltpu.VMEM((pair,) + part, bank.dtype),
            dma((7, n)),
            dma((4, n)),
            dma((4, n)),
            dma((n,)),
            dma((n,)),
            dma((n,)),
            dma((2,)),
            dma((3,)),
        ],
        compiler_params=pltpu.CompilerParams(
            collective_id=0, has_side_effects=True, vmem_limit_bytes=24 << 20
        ),
    )(pick, home, weight.reshape(4, quarter_rows, width), bank)


def body(
    tokens,
    value_weight,
    value_bias,
    down_matrices,
    up_matrices,
    adapter_of_block,
    residency,
    block_length,
):
    block_count, block_rows, model_width = tokens.shape
    rank = down_matrices.shape[2]
    out_width = value_weight.shape[1]
    n = lax.axis_size("seq")
    rep_index = lax.axis_index("rep")
    seq_index = lax.axis_index("seq")
    adapter_ids = jnp.arange(residency.shape[0], dtype=jnp.int32)
    bank_slot = jnp.sum(
        jnp.where(adapter_of_block[:, None] == adapter_ids[None, :], residency[None, :], 0), axis=1
    ).astype(jnp.int32)

    fold = 128 // rank
    down_rows = model_width // n // fold
    up_rows = rank * out_width // n // 128
    pad = -(down_rows + up_rows) % 16
    bank = jnp.concatenate(
        [
            down_matrices[0].reshape(n, fold, down_rows, rank).transpose(0, 2, 1, 3).reshape(n, down_rows, 128),
            up_matrices[0].reshape(n, up_rows, 128),
            jnp.zeros((n, pad, 128), down_matrices.dtype),
        ],
        axis=1,
    )
    weight, parts = gather_all(n, value_weight, bank, bank_slot % n, bank_slot // n, block_count)

    base = jnp.dot(
        tokens.reshape(block_count * block_rows, model_width),
        weight.reshape(model_width, out_width),
        preferred_element_type=jnp.float32,
    ).reshape(block_count, block_rows, out_width)
    down = (
        parts[:, :, :down_rows]
        .reshape(n, block_count, down_rows, fold, rank)
        .transpose(1, 0, 3, 2, 4)
        .reshape(block_count, model_width, rank)
    )
    up = parts[:, :, down_rows : down_rows + up_rows].transpose(1, 0, 2, 3).reshape(block_count, rank, out_width)
    shrunk = jnp.einsum("ctk,ckl->ctl", tokens, down, preferred_element_type=jnp.float32).astype(jnp.bfloat16)
    delta = jnp.einsum("ctl,clv->ctv", shrunk, up, preferred_element_type=jnp.float32)
    positions = seq_index * block_rows + jnp.arange(block_rows, dtype=jnp.int32)
    own_lengths = lax.dynamic_slice_in_dim(block_length, rep_index * block_count, block_count)
    live = positions[None, :] < own_lengths[:, None]
    total = base + value_bias.astype(jnp.float32)[None, None, :] + delta
    return jnp.where(live[:, :, None], total, 0.0).astype(jnp.bfloat16)


def solution(mesh):
    in_specs = (
        P(("outer", "rep"), "seq", None),
        P("seq", None),
        P(),
        P(("outer", "rep", "seq"), None, None),
        P(("outer", "rep", "seq"), None, None),
        P("outer"),
        P("outer"),
        P("outer"),
    )
    out_specs = P(("outer", "rep"), "seq", None)
    return jax.shard_map(body, mesh=mesh, in_specs=in_specs, out_specs=out_specs, check_vma=False)
```

```python
import functools
import jax
import jax.numpy as jnp
from jax import lax
from jax.experimental import pallas as pl
from jax.experimental.pallas import tpu as pltpu
from jax.sharding import PartitionSpec as P

MESH = pl.DeviceIdType.MESH


def grid_of(n):
    near = 1
    while near * near * 4 <= n:
        near *= 2
    return n // near, near


def gather_kernel(
    n, A, B, rank, pick_ref, home_ref, length_ref, bias_ref, w_ref, bank_ref, tok_ref, out_ref,
    w_out, ad_out, tok, acc, low, bank_in, mine, lent, borrowed,
    w_send, w_recv, ad_send, ad_recv, swap_send, swap_recv, lend_sems, local_sems,
):
    o, r, s = lax.axis_index("outer"), lax.axis_index("rep"), lax.axis_index("seq")
    a, b = s // B, s % B
    own, other, sib_own, sib_other = o * 2 + r, (1 - o) * 2 + r, o * 2 + 1 - r, (1 - o) * 2 + 1 - r
    side = {"outer": 1 - o}
    sibling = {"rep": 1 - r}

    barrier = pltpu.get_barrier_semaphore()
    for k in range(1, n):
        pl.semaphore_signal(barrier, inc=1, device_id={"seq": (s + k) % n}, device_id_type=MESH)
    pl.semaphore_signal(barrier, inc=1, device_id=side, device_id_type=MESH)
    pl.semaphore_signal(barrier, inc=1, device_id=sibling, device_id_type=MESH)
    pl.semaphore_wait(barrier, n + 1)

    sent = []

    def start(ok, copy):
        def go():
            copy.start()

        if ok is None:
            go()
        else:
            pl.when(ok)(go)
        sent.append((ok, copy))

    def remote(src, dst, send, recv, device):
        return pltpu.make_async_remote_copy(
            src_ref=src, dst_ref=dst, send_sem=send, recv_sem=recv, device_id=device, device_id_type=MESH
        )

    def both(x, y):
        return x if y is None else (y if x is None else jnp.logical_and(x, y))

    def far(step):
        at = a + step
        ok = jnp.logical_and(at >= 0, at < A)
        return ok, jnp.clip(at, 0, A - 1)

    def near(step):
        at = b + step
        ok = jnp.logical_and(at >= 0, at < B)
        return ok, jnp.clip(at, 0, B - 1)

    class Flow:
        def __init__(self, out, send, recv, wide):
            self.out, self.send, self.recv, self.wide = out, send, recv, wide

        def put(self, ok, src, shard, lane, device):
            start(ok, remote(src, self.out(shard), self.send.at[lane, shard], self.recv(shard), device))

        def far_put(self, ok, src, shard, step):
            there, row = far(step)
            self.put(both(ok, there), src, shard, 0 if step < 0 else 1, {"seq": row * B + b})

        def near_put(self, ok, src, shard, step):
            there, col = near(step)
            self.put(both(ok, there), src, shard, 2 if step < 0 else 3, {"seq": a * B + col})

        def arrive(self, ok, shard):
            block = self.out(shard)

            @pl.when(ok)
            def _():
                pltpu.make_async_copy(block, block, self.recv(shard)).wait()

            return block

        def widen(self, ok, src, shard):
            if self.wide:
                self.put(ok, src, shard, 4, side)
                self.put(ok, src, shard, 5, sibling)

        def begin(self, src):
            for step in (-1, 1):
                self.far_put(None, src, s, step)
            for step in (-1, 1):
                self.near_put(None, src, s, step)

        def wave(self, d):
            rows = []
            for sign in (-1, 1) if d else (1,):
                ok, row = far(sign * d)
                rows.append((ok if d else None, row))
                if d:
                    shard = row * B + b
                    src = self.arrive(ok, shard)
                    self.far_put(ok, src, shard, -sign)
                    for step in (-1, 1):
                        self.near_put(ok, src, shard, step)
                    self.widen(ok, src, shard)
            for row_ok, row in rows:
                for e in range(1, B):
                    for sign in (-1, 1):
                        there, col = near(sign * e)
                        ok = both(row_ok, there)
                        shard = row * B + col
                        src = self.arrive(ok, shard)
                        if e < B - 1:
                            self.near_put(ok, src, shard, -sign)
                        self.widen(ok, src, shard)

        def shards(self, d):
            found = []
            for sign in (-1, 1) if d else (1,):
                row_ok, row = far(sign * d)
                if d:
                    found.append((row_ok, row * B + b))
                for e in range(1, B):
                    for near_sign in (-1, 1):
                        there, col = near(near_sign * e)
                        found.append((both(row_ok if d else None, there), row * B + col))
            return found

    weights = Flow(lambda k: w_out.at[k, own], w_send, lambda k: w_recv.at[own, k], True)
    adapters = Flow(lambda k: ad_out.at[k], ad_send, lambda k: ad_recv.at[k], False)

    def cross(d):
        for ok, shard in weights.shards(d):
            block = w_out.at[shard, other]

            @pl.when(ok)
            def _(block=block, shard=shard):
                pltpu.make_async_copy(block, block, w_recv.at[other, shard]).wait()

            start(ok, remote(block, block, w_send.at[6, shard], w_recv.at[other, shard], sibling))

    pair, depth, width = mine.shape[0], tok.shape[1] // n, acc.shape[1]
    block_rows = tok.shape[0] // pair
    fold = 128 // rank
    down_rows = depth // fold
    groups = width // 128
    tile = min(width, 256)

    def columns(shard):
        return pl.ds(pl.multiple_of(shard * depth, 128), depth)

    def project(shard, first=False):
        @pl.loop(0, width // tile)
        def _(i):
            at = pl.ds(pl.multiple_of(i * tile, tile), tile)
            term = jnp.dot(
                tok[:, columns(shard)],
                w_out[shard, :, :, at].reshape(depth, tile),
                preferred_element_type=jnp.float32,
            )
            acc[:, at] = term + (bias_ref[:, at].astype(jnp.float32) if first else acc[:, at])

    def reach(d):
        return 1 + jnp.minimum(a, d) + jnp.minimum(A - 1 - a, d)

    def projects(d):
        low_end = B * reach(d - 1) if d else 1

        @pl.loop(low_end, B * reach(d))
        def _(j):
            k = j // B
            edge = jnp.minimum(a, A - 1 - a)
            swing = jnp.where(k % 2 == 1, a - (k + 1) // 2, a + k // 2)
            row = jnp.where(k <= 2 * edge, swing, jnp.where(2 * a < A, k, A - 1 - k))
            shard = row * B + (b + j % B) % B
            for quarter in (sib_own, sib_other):
                block = w_out.at[shard, quarter]
                pltpu.make_async_copy(block, block, w_recv.at[quarter, shard]).wait()
            project(shard)

    def shrink():
        low[...] = jnp.zeros_like(low)

        @pl.loop(0, n)
        def _(k):
            for c in range(pair):
                rows = tok[c * block_rows : (c + 1) * block_rows, columns(k)]
                down = ad_out[k, c, :down_rows]
                for f in range(fold):
                    low[c, f] += jnp.dot(
                        rows[:, f * down_rows : (f + 1) * down_rows], down, preferred_element_type=jnp.float32
                    )

    for k in range(1, n):
        to = (s + k) % n
        start(None, remote(bank_ref.at[to], bank_in.at[s], swap_send.at[k], swap_recv.at[s], {"seq": to}))
    weights.begin(w_ref.at[own])
    kept = pltpu.make_async_copy(bank_ref.at[s], bank_in.at[s], local_sems.at[0])
    kept.start()
    whole = pltpu.make_async_copy(w_ref, w_out.at[s], local_sems.at[1])
    whole.start()
    held = pltpu.make_async_copy(tok_ref, tok, local_sems.at[3])
    held.start()

    whole.wait()
    held.wait()
    project(s, True)
    weights.wave(0)
    if A > 1:
        weights.wave(1)

    kept.wait()
    for k in range(1, n):
        sender = (s + k) % n
        part = bank_in.at[sender]
        pltpu.make_async_copy(part, part, swap_recv.at[sender]).wait()
    for c in range(pair):
        lent[c] = bank_in[pick_ref[(1 - r) * pair + c]]
    lend = remote(lent, borrowed, lend_sems.at[0], lend_sems.at[1], sibling)
    lend.start()
    lend.wait()
    for c in range(pair):
        here = home_ref[r * pair + c] == r
        mine[c] = jnp.where(here, bank_in[pick_ref[r * pair + c]], borrowed[c])
    adapters.begin(mine)
    stored = pltpu.make_async_copy(mine, ad_out.at[s], local_sems.at[2])
    stored.start()

    cross(0)
    for d in range(2, A):
        weights.wave(d)
        adapters.wave(d - 2)
        cross(d - 1)
        projects(d - 2)
    for d in range(max(A - 2, 0), A):
        adapters.wave(d)
    if A > 1:
        projects(A - 2)
    stored.wait()
    shrink()
    if A > 1:
        cross(A - 1)
    projects(A - 1)

    for c in range(pair):
        rows = slice(c * block_rows, (c + 1) * block_rows)
        narrow = sum(low[c, f][:, f * rank : (f + 1) * rank] for f in range(fold)).astype(jnp.bfloat16)
        at = s * block_rows + lax.broadcasted_iota(jnp.int32, (block_rows, 128), 0)
        live = at < length_ref[r * pair + c]
        for g in range(groups):
            pieces = [ad_out[k, c, down_rows : down_rows + rank * groups // n] for k in range(g, n, groups)]
            up = pieces[0]
            if len(pieces) > 1:
                up = jnp.concatenate([x.astype(jnp.float32) for x in pieces], axis=0).astype(jnp.bfloat16)
            delta = jnp.dot(narrow, up, preferred_element_type=jnp.float32)
            cut = slice(g * 128, (g + 1) * 128)
            out_ref[rows, cut] = jnp.where(live, acc[rows, cut] + delta, 0.0).astype(out_ref.dtype)
    for ok, copy in sent:
        if ok is None:
            copy.wait_send()
        else:
            pl.when(ok)(copy.wait_send)


def run(n, tokens, weight, bias, bank, pick, home, length, pair, rank):
    A, B = grid_of(n)
    quarter_rows, width = weight.shape[0] // 4, weight.shape[1]
    part = bank.shape[1:]
    rows = tokens.shape[0]
    any_space = pl.BlockSpec(memory_space=pl.ANY)
    scalars = pl.BlockSpec(memory_space=pltpu.SMEM)
    vmem = pl.BlockSpec(memory_space=pltpu.VMEM)
    dma = pltpu.SemaphoreType.DMA
    return pl.pallas_call(
        functools.partial(gather_kernel, n, A, B, rank),
        out_shape=jax.ShapeDtypeStruct((rows, width), jnp.bfloat16),
        in_specs=[scalars, scalars, scalars, vmem, any_space, any_space, any_space],
        out_specs=vmem,
        scratch_shapes=[
            pltpu.VMEM((n, 4, quarter_rows, width), weight.dtype),
            pltpu.VMEM((n, pair) + part, bank.dtype),
            pltpu.VMEM(tokens.shape, tokens.dtype),
            pltpu.VMEM((rows, width), jnp.float32),
            pltpu.VMEM((pair, 128 // rank, rows // pair, 128), jnp.float32),
            pltpu.VMEM((n,) + part, bank.dtype),
            pltpu.VMEM((pair,) + part, bank.dtype),
            pltpu.VMEM((pair,) + part, bank.dtype),
            pltpu.VMEM((pair,) + part, bank.dtype),
            dma((7, n)),
            dma((4, n)),
            dma((4, n)),
            dma((n,)),
            dma((n,)),
            dma((n,)),
            dma((2,)),
            dma((4,)),
        ],
        compiler_params=pltpu.CompilerParams(
            collective_id=0, has_side_effects=True, vmem_limit_bytes=44 << 20
        ),
    )(pick, home, length, bias, weight.reshape(4, quarter_rows, width), bank, tokens)


def body(
    tokens,
    value_weight,
    value_bias,
    down_matrices,
    up_matrices,
    adapter_of_block,
    residency,
    block_length,
):
    block_count, block_rows, model_width = tokens.shape
    rank = down_matrices.shape[2]
    out_width = value_weight.shape[1]
    n = lax.axis_size("seq")
    adapter_ids = jnp.arange(residency.shape[0], dtype=jnp.int32)
    bank_slot = jnp.sum(
        jnp.where(adapter_of_block[:, None] == adapter_ids[None, :], residency[None, :], 0), axis=1
    ).astype(jnp.int32)

    fold = 128 // rank
    down_rows = model_width // n // fold
    groups = out_width // 128
    up_rows = rank * groups // n
    pad = -(down_rows + up_rows) % 16
    bank = jnp.concatenate(
        [
            down_matrices[0].reshape(n, fold, down_rows, rank).transpose(0, 2, 1, 3).reshape(n, down_rows, 128),
            up_matrices[0].reshape(n // groups, up_rows, groups, 128).transpose(0, 2, 1, 3).reshape(n, up_rows, 128),
            jnp.zeros((n, pad, 128), down_matrices.dtype),
        ],
        axis=1,
    )
    out = run(
        n,
        tokens.reshape(block_count * block_rows, model_width),
        value_weight,
        value_bias.reshape(1, out_width),
        bank,
        bank_slot % n,
        bank_slot // n,
        block_length,
        block_count,
        rank,
    )
    return out.reshape(block_count, block_rows, out_width)


def solution(mesh):
    in_specs = (
        P(("outer", "rep"), "seq", None),
        P("seq", None),
        P(),
        P(("outer", "rep", "seq"), None, None),
        P(("outer", "rep", "seq"), None, None),
        P("outer"),
        P("outer"),
        P("outer"),
    )
    out_specs = P(("outer", "rep"), "seq", None)
    return jax.shard_map(body, mesh=mesh, in_specs=in_specs, out_specs=out_specs, check_vma=False)
```

```python
import functools
import jax
import jax.numpy as jnp
from jax import lax
from jax.experimental import pallas as pl
from jax.experimental.pallas import tpu as pltpu
from jax.sharding import PartitionSpec as P

MESH = pl.DeviceIdType.MESH
SLICE_ROWS = 256


def grid_of(n):
    near = 1
    while near * near * 4 <= n:
        near *= 2
    return n // near, near


def gather_kernel(
    n, A, B, S, rank, pick_ref, home_ref, length_ref, bias_ref, w_ref, bank_ref, tok_ref, out_ref,
    w_out, ad_out, tok, acc, low, bank_in, mine, lent, borrowed,
    w_send, w_recv, ad_send, ad_recv, swap_send, swap_recv, lend_sems, local_sems,
):
    o, r, s = lax.axis_index("outer"), lax.axis_index("rep"), lax.axis_index("seq")
    a, b = s // B, s % B
    own, other, sib_own, sib_other = o * 2 + r, (1 - o) * 2 + r, o * 2 + 1 - r, (1 - o) * 2 + 1 - r
    side = {"outer": 1 - o}
    sibling = {"rep": 1 - r}

    barrier = pltpu.get_barrier_semaphore()
    for k in range(1, n):
        pl.semaphore_signal(barrier, inc=1, device_id={"seq": (s + k) % n}, device_id_type=MESH)
    pl.semaphore_signal(barrier, inc=1, device_id=side, device_id_type=MESH)
    pl.semaphore_signal(barrier, inc=1, device_id=sibling, device_id_type=MESH)
    pl.semaphore_wait(barrier, n + 1)

    closing = []

    def start(ok, make, p):
        def go():
            if closing:
                make(p).wait_send()
            else:
                make(p).start()

        if ok is None:
            go()
        else:
            pl.when(ok)(go)

    def remote(src, dst, send, recv, device):
        return pltpu.make_async_remote_copy(
            src_ref=src, dst_ref=dst, send_sem=send, recv_sem=recv, device_id=device, device_id_type=MESH
        )

    def both(x, y):
        return x if y is None else (y if x is None else jnp.logical_and(x, y))

    def far(step):
        at = a + step
        ok = jnp.logical_and(at >= 0, at < A)
        return ok, jnp.clip(at, 0, A - 1)

    def near(step):
        at = b + step
        ok = jnp.logical_and(at >= 0, at < B)
        return ok, jnp.clip(at, 0, B - 1)

    class Flow:
        def __init__(self, out, send, recv, wide, slices):
            self.out, self.send, self.recv, self.wide, self.slices = out, send, recv, wide, slices

        def put(self, ok, src, shard, lane, device, p):
            def make(q):
                return remote(src(q), self.out(shard, q), self.send.at[lane, shard, q], self.recv(shard, q), device)

            start(ok, make, p)

        def far_put(self, ok, src, shard, step, p):
            there, row = far(step)
            self.put(both(ok, there), src, shard, 0 if step < 0 else 1, {"seq": row * B + b}, p)

        def near_put(self, ok, src, shard, step, p):
            there, col = near(step)
            self.put(both(ok, there), src, shard, 2 if step < 0 else 3, {"seq": a * B + col}, p)

        def arrive(self, ok, shard, p):
            if not closing:

                @pl.when(ok)
                def _():
                    block = self.out(shard, p)
                    pltpu.make_async_copy(block, block, self.recv(shard, p)).wait()

            return lambda q: self.out(shard, q)

        def widen(self, ok, src, shard, p):
            if self.wide:
                self.put(ok, src, shard, 4, side, p)
                self.put(ok, src, shard, 5, sibling, p)

        def begin(self, src):
            @pl.loop(0, self.slices)
            def _(p):
                for step in (-1, 1):
                    self.far_put(None, src, s, step, p)
                for step in (-1, 1):
                    self.near_put(None, src, s, step, p)

        def wave(self, d, p):
            rows = []
            for sign in (-1, 1) if d else (1,):
                ok, row = far(sign * d)
                rows.append((ok if d else None, row))
                if d:
                    shard = row * B + b
                    src = self.arrive(ok, shard, p)
                    self.far_put(ok, src, shard, -sign, p)
                    for step in (-1, 1):
                        self.near_put(ok, src, shard, step, p)
                    self.widen(ok, src, shard, p)
            for row_ok, row in rows:
                for e in range(1, B):
                    for sign in (-1, 1):
                        there, col = near(sign * e)
                        ok = both(row_ok, there)
                        shard = row * B + col
                        src = self.arrive(ok, shard, p)
                        if e < B - 1:
                            self.near_put(ok, src, shard, -sign, p)
                        self.widen(ok, src, shard, p)

        def shards(self, d):
            found = []
            for sign in (-1, 1) if d else (1,):
                row_ok, row = far(sign * d)
                if d:
                    found.append((row_ok, row * B + b))
                for e in range(1, B):
                    for near_sign in (-1, 1):
                        there, col = near(near_sign * e)
                        found.append((both(row_ok if d else None, there), row * B + col))
            return found

    slice_rows = w_out.shape[2] // S

    def cut(ref, p):
        return ref.at[pl.ds(p * slice_rows, slice_rows)]

    weights = Flow(
        lambda k, p: cut(w_out.at[k, own], p), w_send, lambda k, p: w_recv.at[own, k, p], True, S
    )
    adapters = Flow(lambda k, p: ad_out.at[k, p], ad_send, lambda k, p: ad_recv.at[k, p], False, mine.shape[0])

    def cross(d, p):
        for ok, shard in weights.shards(d):

            if not closing:

                @pl.when(ok)
                def _(shard=shard):
                    block = cut(w_out.at[shard, other], p)
                    pltpu.make_async_copy(block, block, w_recv.at[other, shard, p]).wait()

            def make(q, shard=shard):
                block = cut(w_out.at[shard, other], q)
                return remote(block, block, w_send.at[6, shard, q], w_recv.at[other, shard, q], sibling)

            start(ok, make, p)

    def steps(flow, *ds):
        @pl.loop(0, flow.slices)
        def _(p):
            for d in ds:
                flow.wave(d, p)

    def crosses(d):
        @pl.loop(0, S)
        def _(p):
            cross(d, p)

    pair, depth, width = mine.shape[0], tok.shape[1] // n, acc.shape[1]
    block_rows = tok.shape[0] // pair
    fold = 128 // rank
    down_rows = depth // fold
    groups = width // 128
    tile = min(width, 256)

    def columns(shard):
        return pl.ds(pl.multiple_of(shard * depth, 128), depth)

    def project(shard, first=False):
        @pl.loop(0, width // tile)
        def _(i):
            at = pl.ds(pl.multiple_of(i * tile, tile), tile)
            term = jnp.dot(
                tok[:, columns(shard)],
                w_out[shard, :, :, at].reshape(depth, tile),
                preferred_element_type=jnp.float32,
            )
            acc[:, at] = term + (bias_ref[:, at].astype(jnp.float32) if first else acc[:, at])

    def reach(d):
        return 1 + jnp.minimum(a, d) + jnp.minimum(A - 1 - a, d)

    def projects(d):
        low_end = B * reach(d - 1) if d else 1

        @pl.loop(low_end, B * reach(d))
        def _(j):
            k = j // B
            edge = jnp.minimum(a, A - 1 - a)
            swing = jnp.where(k % 2 == 1, a - (k + 1) // 2, a + k // 2)
            row = jnp.where(k <= 2 * edge, swing, jnp.where(2 * a < A, k, A - 1 - k))
            shard = row * B + (b + j % B) % B
            for quarter in (sib_own, sib_other):
                for p in range(S):
                    block = cut(w_out.at[shard, quarter], p)
                    pltpu.make_async_copy(block, block, w_recv.at[quarter, shard, p]).wait()
            project(shard)

    def shrink():
        low[...] = jnp.zeros_like(low)

        @pl.loop(0, n)
        def _(k):
            for c in range(pair):
                rows = tok[c * block_rows : (c + 1) * block_rows, columns(k)]
                down = ad_out[k, c, :down_rows]
                for f in range(fold):
                    low[c, f] += jnp.dot(
                        rows[:, f * down_rows : (f + 1) * down_rows], down, preferred_element_type=jnp.float32
                    )

    weights.begin(lambda p: cut(w_ref.at[own], p))
    whole = pltpu.make_async_copy(w_ref, w_out.at[s], local_sems.at[1])
    whole.start()
    kept = pltpu.make_async_copy(bank_ref.at[s], bank_in.at[s], local_sems.at[0])
    kept.start()
    held = pltpu.make_async_copy(tok_ref, tok, local_sems.at[3])
    held.start()

    def swap(k):
        to = (s + k) % n
        return remote(bank_ref.at[to], bank_in.at[s], swap_send.at[k], swap_recv.at[s], {"seq": to})

    @pl.loop(1, n)
    def _(k):
        swap(k).start()

    steps(weights, *range(min(2, A)))
    whole.wait()
    held.wait()
    project(s, True)

    kept.wait()
    for k in range(1, n):
        sender = (s + k) % n
        part = bank_in.at[sender]
        pltpu.make_async_copy(part, part, swap_recv.at[sender]).wait()
    for c in range(pair):
        lent[c] = bank_in[pick_ref[(1 - r) * pair + c]]
    lend = remote(lent, borrowed, lend_sems.at[0], lend_sems.at[1], sibling)
    lend.start()
    lend.wait()
    for c in range(pair):
        here = home_ref[r * pair + c] == r
        mine[c] = jnp.where(here, bank_in[pick_ref[r * pair + c]], borrowed[c])
    adapters.begin(lambda p: mine.at[p])
    stored = pltpu.make_async_copy(mine, ad_out.at[s], local_sems.at[2])
    stored.start()

    crosses(0)
    for d in range(2, A):
        steps(weights, d)
        steps(adapters, d - 2)
        crosses(d - 1)
        projects(d - 2)
    steps(adapters, *range(max(A - 2, 0), A))
    if A > 1:
        projects(A - 2)
    stored.wait()
    shrink()
    if A > 1:
        crosses(A - 1)
    projects(A - 1)

    for c in range(pair):
        rows = slice(c * block_rows, (c + 1) * block_rows)
        narrow = sum(low[c, f][:, f * rank : (f + 1) * rank] for f in range(fold)).astype(jnp.bfloat16)
        at = s * block_rows + lax.broadcasted_iota(jnp.int32, (block_rows, 128), 0)
        live = at < length_ref[r * pair + c]
        for g in range(groups):
            pieces = [ad_out[k, c, down_rows : down_rows + rank * groups // n] for k in range(g, n, groups)]
            up = pieces[0]
            if len(pieces) > 1:
                up = jnp.concatenate([x.astype(jnp.float32) for x in pieces], axis=0).astype(jnp.bfloat16)
            delta = jnp.dot(narrow, up, preferred_element_type=jnp.float32)
            span = slice(g * 128, (g + 1) * 128)
            out_ref[rows, span] = jnp.where(live, acc[rows, span] + delta, 0.0).astype(out_ref.dtype)

    @pl.loop(1, n)
    def _(k):
        swap(k).wait_send()

    closing.append(True)
    weights.begin(lambda p: cut(w_ref.at[own], p))
    adapters.begin(lambda p: mine.at[p])
    steps(weights, *range(A))
    steps(adapters, *range(A))
    for d in range(A):
        crosses(d)


def run(n, tokens, weight, bias, bank, pick, home, length, pair, rank):
    A, B = grid_of(n)
    quarter_rows, width = weight.shape[0] // 4, weight.shape[1]
    S = max(1, quarter_rows // SLICE_ROWS)
    part = bank.shape[1:]
    rows = tokens.shape[0]
    any_space = pl.BlockSpec(memory_space=pl.ANY)
    scalars = pl.BlockSpec(memory_space=pltpu.SMEM)
    vmem = pl.BlockSpec(memory_space=pltpu.VMEM)
    dma = pltpu.SemaphoreType.DMA
    return pl.pallas_call(
        functools.partial(gather_kernel, n, A, B, S, rank),
        out_shape=jax.ShapeDtypeStruct((rows, width), jnp.bfloat16),
        in_specs=[scalars, scalars, scalars, vmem, any_space, any_space, any_space],
        out_specs=vmem,
        scratch_shapes=[
            pltpu.VMEM((n, 4, quarter_rows, width), weight.dtype),
            pltpu.VMEM((n, pair) + part, bank.dtype),
            pltpu.VMEM(tokens.shape, tokens.dtype),
            pltpu.VMEM((rows, width), jnp.float32),
            pltpu.VMEM((pair, 128 // rank, rows // pair, 128), jnp.float32),
            pltpu.VMEM((n,) + part, bank.dtype),
            pltpu.VMEM((pair,) + part, bank.dtype),
            pltpu.VMEM((pair,) + part, bank.dtype),
            pltpu.VMEM((pair,) + part, bank.dtype),
            dma((7, n, S)),
            dma((4, n, S)),
            dma((4, n, pair)),
            dma((n, pair)),
            dma((n,)),
            dma((n,)),
            dma((2,)),
            dma((4,)),
        ],
        compiler_params=pltpu.CompilerParams(
            collective_id=0, has_side_effects=True, vmem_limit_bytes=44 << 20
        ),
    )(pick, home, length, bias, weight.reshape(4, quarter_rows, width), bank, tokens)


def body(
    tokens,
    value_weight,
    value_bias,
    down_matrices,
    up_matrices,
    adapter_of_block,
    residency,
    block_length,
):
    block_count, block_rows, model_width = tokens.shape
    rank = down_matrices.shape[2]
    out_width = value_weight.shape[1]
    n = lax.axis_size("seq")
    adapter_ids = jnp.arange(residency.shape[0], dtype=jnp.int32)
    bank_slot = jnp.sum(
        jnp.where(adapter_of_block[:, None] == adapter_ids[None, :], residency[None, :], 0), axis=1
    ).astype(jnp.int32)

    fold = 128 // rank
    down_rows = model_width // n // fold
    groups = out_width // 128
    up_rows = rank * groups // n
    pad = -(down_rows + up_rows) % 16
    bank = jnp.concatenate(
        [
            down_matrices[0].reshape(n, fold, down_rows, rank).transpose(0, 2, 1, 3).reshape(n, down_rows, 128),
            up_matrices[0].reshape(n // groups, up_rows, groups, 128).transpose(0, 2, 1, 3).reshape(n, up_rows, 128),
            jnp.zeros((n, pad, 128), down_matrices.dtype),
        ],
        axis=1,
    )
    out = run(
        n,
        tokens.reshape(block_count * block_rows, model_width),
        value_weight,
        value_bias.reshape(1, out_width),
        bank,
        bank_slot % n,
        bank_slot // n,
        block_length,
        block_count,
        rank,
    )
    return out.reshape(block_count, block_rows, out_width)


def solution(mesh):
    in_specs = (
        P(("outer", "rep"), "seq", None),
        P("seq", None),
        P(),
        P(("outer", "rep", "seq"), None, None),
        P(("outer", "rep", "seq"), None, None),
        P("outer"),
        P("outer"),
        P("outer"),
    )
    out_specs = P(("outer", "rep"), "seq", None)
    return jax.shard_map(body, mesh=mesh, in_specs=in_specs, out_specs=out_specs, check_vma=False)
```

```python
import functools
import jax
import jax.numpy as jnp
from jax import lax
from jax.experimental import pallas as pl
from jax.experimental.pallas import tpu as pltpu
from jax.sharding import PartitionSpec as P

MESH = pl.DeviceIdType.MESH
SLICE_ROWS = 256


def grid_of(n):
    near = 1
    while near * near * 4 <= n:
        near *= 2
    return n // near, near


def gather_kernel(
    n, A, B, S, rank, pick_ref, home_ref, length_ref, bias_ref, w_ref, bank_ref, tok_ref, out_ref,
    w_out, ad_out, tok, acc, low, bank_in, mine, lent, borrowed,
    w_send, w_recv, ad_send, ad_recv, swap_send, swap_recv, lend_sems, local_sems,
):
    o, r, s = lax.axis_index("outer"), lax.axis_index("rep"), lax.axis_index("seq")
    a, b = s // B, s % B
    own, other, sib_own, sib_other = o * 2 + r, (1 - o) * 2 + r, o * 2 + 1 - r, (1 - o) * 2 + 1 - r
    side = {"outer": 1 - o}
    sibling = {"rep": 1 - r}

    barrier = pltpu.get_barrier_semaphore()
    for k in range(1, n):
        pl.semaphore_signal(barrier, inc=1, device_id={"seq": (s + k) % n}, device_id_type=MESH)
    pl.semaphore_signal(barrier, inc=1, device_id=side, device_id_type=MESH)
    pl.semaphore_signal(barrier, inc=1, device_id=sibling, device_id_type=MESH)
    pl.semaphore_wait(barrier, n + 1)

    closing = []

    def start(ok, make, p):
        def go():
            if closing:
                make(p).wait_send()
            else:
                make(p).start()

        if ok is None:
            go()
        else:
            pl.when(ok)(go)

    def remote(src, dst, send, recv, device):
        return pltpu.make_async_remote_copy(
            src_ref=src, dst_ref=dst, send_sem=send, recv_sem=recv, device_id=device, device_id_type=MESH
        )

    def both(x, y):
        return x if y is None else (y if x is None else jnp.logical_and(x, y))

    def far(step):
        at = a + step
        ok = jnp.logical_and(at >= 0, at < A)
        return ok, jnp.clip(at, 0, A - 1)

    def near(step):
        at = b + step
        ok = jnp.logical_and(at >= 0, at < B)
        return ok, jnp.clip(at, 0, B - 1)

    class Flow:
        def __init__(self, out, send, recv, wide, slices):
            self.out, self.send, self.recv, self.wide, self.slices = out, send, recv, wide, slices

        def put(self, ok, src, shard, lane, device, p):
            def make(q):
                return remote(src(q), self.out(shard, q), self.send.at[lane, shard, q], self.recv(shard, q), device)

            start(ok, make, p)

        def far_put(self, ok, src, shard, step, p):
            there, row = far(step)
            self.put(both(ok, there), src, shard, 0 if step < 0 else 1, {"seq": row * B + b}, p)

        def near_put(self, ok, src, shard, step, p):
            there, col = near(step)
            self.put(both(ok, there), src, shard, 2 if step < 0 else 3, {"seq": a * B + col}, p)

        def arrive(self, ok, shard, p):
            if not closing:

                @pl.when(ok)
                def _():
                    block = self.out(shard, p)
                    pltpu.make_async_copy(block, block, self.recv(shard, p)).wait()

            return lambda q: self.out(shard, q)

        def widen(self, ok, src, shard, p):
            if self.wide:
                self.put(ok, src, shard, 4, side, p)
                self.put(ok, src, shard, 5, sibling, p)

        def begin(self, src):
            @pl.loop(0, self.slices)
            def _(p):
                for step in (-1, 1):
                    self.far_put(None, src, s, step, p)
                for step in (-1, 1):
                    self.near_put(None, src, s, step, p)

        def wave(self, d, p):
            rows = []
            for sign in (-1, 1) if d else (1,):
                ok, row = far(sign * d)
                rows.append((ok if d else None, row))
                if d:
                    shard = row * B + b
                    src = self.arrive(ok, shard, p)
                    self.far_put(ok, src, shard, -sign, p)
                    for step in (-1, 1):
                        self.near_put(ok, src, shard, step, p)
                    self.widen(ok, src, shard, p)
            for row_ok, row in rows:
                for e in range(1, B):
                    for sign in (-1, 1):
                        there, col = near(sign * e)
                        ok = both(row_ok, there)
                        shard = row * B + col
                        src = self.arrive(ok, shard, p)
                        if e < B - 1:
                            self.near_put(ok, src, shard, -sign, p)
                        self.widen(ok, src, shard, p)

        def shards(self, d):
            found = []
            for sign in (-1, 1) if d else (1,):
                row_ok, row = far(sign * d)
                if d:
                    found.append((row_ok, row * B + b))
                for e in range(1, B):
                    for near_sign in (-1, 1):
                        there, col = near(near_sign * e)
                        found.append((both(row_ok if d else None, there), row * B + col))
            return found

    slice_rows = w_out.shape[2] // S

    def cut(ref, p):
        return ref.at[pl.ds(p * slice_rows, slice_rows)]

    weights = Flow(
        lambda k, p: cut(w_out.at[k, own], p), w_send, lambda k, p: w_recv.at[own, k, p], True, S
    )
    adapters = Flow(lambda k, p: ad_out.at[k, p], ad_send, lambda k, p: ad_recv.at[k, p], False, mine.shape[0])

    def cross(d, p):
        for ok, shard in weights.shards(d):

            if not closing:

                @pl.when(ok)
                def _(shard=shard):
                    block = cut(w_out.at[shard, other], p)
                    pltpu.make_async_copy(block, block, w_recv.at[other, shard, p]).wait()

            def make(q, shard=shard):
                block = cut(w_out.at[shard, other], q)
                return remote(block, block, w_send.at[6, shard, q], w_recv.at[other, shard, q], sibling)

            start(ok, make, p)

    def steps(flow, *ds):
        @pl.loop(0, flow.slices)
        def _(p):
            for d in ds:
                flow.wave(d, p)

    def crosses(d):
        @pl.loop(0, S)
        def _(p):
            cross(d, p)

    pair, depth, width = mine.shape[0], tok.shape[1] // n, acc.shape[1]
    block_rows = tok.shape[0] // pair
    fold = 128 // rank
    down_rows = depth // fold
    groups = width // 128
    tile = min(width, 256)

    def columns(shard):
        return pl.ds(pl.multiple_of(shard * depth, 128), depth)

    def project(shard, first=False):
        @pl.loop(0, width // tile)
        def _(i):
            at = pl.ds(pl.multiple_of(i * tile, tile), tile)
            term = jnp.dot(
                tok[:, columns(shard)],
                w_out[shard, :, :, at].reshape(depth, tile),
                preferred_element_type=jnp.float32,
            )
            acc[:, at] = term + (bias_ref[:, at].astype(jnp.float32) if first else acc[:, at])

    def reach(d):
        return 1 + jnp.minimum(a, d) + jnp.minimum(A - 1 - a, d)

    def projects(d):
        low_end = B * reach(d - 1) if d else 1

        @pl.loop(low_end, B * reach(d))
        def _(j):
            k = j // B
            edge = jnp.minimum(a, A - 1 - a)
            swing = jnp.where(k % 2 == 1, a - (k + 1) // 2, a + k // 2)
            row = jnp.where(k <= 2 * edge, swing, jnp.where(2 * a < A, k, A - 1 - k))
            shard = row * B + (b + j % B) % B
            for quarter in (sib_own, sib_other):
                for p in range(S):
                    block = cut(w_out.at[shard, quarter], p)
                    pltpu.make_async_copy(block, block, w_recv.at[quarter, shard, p]).wait()
            project(shard)

    def shrink():
        low[...] = jnp.zeros_like(low)

        @pl.loop(0, n)
        def _(k):
            for c in range(pair):
                rows = tok[c * block_rows : (c + 1) * block_rows, columns(k)]
                down = ad_out[k, c, :down_rows]
                for f in range(fold):
                    low[c, f] += jnp.dot(
                        rows[:, f * down_rows : (f + 1) * down_rows], down, preferred_element_type=jnp.float32
                    )

    weights.begin(lambda p: cut(w_ref.at[own], p))
    whole = pltpu.make_async_copy(w_ref, w_out.at[s], local_sems.at[1])
    whole.start()
    kept = pltpu.make_async_copy(bank_ref.at[s], bank_in.at[s], local_sems.at[0])
    kept.start()
    held = pltpu.make_async_copy(tok_ref, tok, local_sems.at[3])
    held.start()

    def swap(k):
        to = (s + k) % n
        return remote(bank_ref.at[to], bank_in.at[s], swap_send.at[k], swap_recv.at[s], {"seq": to})

    @pl.loop(1, n)
    def _(k):
        swap(k).start()

    steps(weights, *range(min(2, A)))
    whole.wait()
    held.wait()
    project(s, True)

    kept.wait()
    for k in range(1, n):
        sender = (s + k) % n
        part = bank_in.at[sender]
        pltpu.make_async_copy(part, part, swap_recv.at[sender]).wait()
    for c in range(pair):
        lent[c] = bank_in[pick_ref[(1 - r) * pair + c]]
    lend = remote(lent, borrowed, lend_sems.at[0], lend_sems.at[1], sibling)
    lend.start()
    lend.wait()
    for c in range(pair):
        here = home_ref[r * pair + c] == r
        mine[c] = jnp.where(here, bank_in[pick_ref[r * pair + c]], borrowed[c])
    adapters.begin(lambda p: mine.at[p])
    stored = pltpu.make_async_copy(mine, ad_out.at[s], local_sems.at[2])
    stored.start()

    crosses(0)
    for d in range(2, A):
        steps(weights, d)
        steps(adapters, d - 2)
        crosses(d - 1)
        projects(d - 2)
    steps(adapters, *range(max(A - 2, 0), A))
    if A > 1:
        crosses(A - 1)
        projects(A - 2)
    stored.wait()
    shrink()
    projects(A - 1)

    for c in range(pair):
        rows = slice(c * block_rows, (c + 1) * block_rows)
        narrow = sum(low[c, f][:, f * rank : (f + 1) * rank] for f in range(fold)).astype(jnp.bfloat16)
        at = s * block_rows + lax.broadcasted_iota(jnp.int32, (block_rows, 128), 0)
        live = at < length_ref[r * pair + c]
        for g in range(groups):
            pieces = [ad_out[k, c, down_rows : down_rows + rank * groups // n] for k in range(g, n, groups)]
            up = pieces[0]
            if len(pieces) > 1:
                up = jnp.concatenate([x.astype(jnp.float32) for x in pieces], axis=0).astype(jnp.bfloat16)
            delta = jnp.dot(narrow, up, preferred_element_type=jnp.float32)
            span = slice(g * 128, (g + 1) * 128)
            out_ref[rows, span] = jnp.where(live, acc[rows, span] + delta, 0.0).astype(out_ref.dtype)

    @pl.loop(1, n)
    def _(k):
        swap(k).wait_send()

    closing.append(True)
    weights.begin(lambda p: cut(w_ref.at[own], p))
    adapters.begin(lambda p: mine.at[p])
    steps(weights, *range(A))
    steps(adapters, *range(A))
    for d in range(A):
        crosses(d)


def run(n, tokens, weight, bias, bank, pick, home, length, pair, rank):
    A, B = grid_of(n)
    quarter_rows, width = weight.shape[0] // 4, weight.shape[1]
    S = max(1, quarter_rows // SLICE_ROWS)
    part = bank.shape[1:]
    rows = tokens.shape[0]
    any_space = pl.BlockSpec(memory_space=pl.ANY)
    scalars = pl.BlockSpec(memory_space=pltpu.SMEM)
    vmem = pl.BlockSpec(memory_space=pltpu.VMEM)
    dma = pltpu.SemaphoreType.DMA
    return pl.pallas_call(
        functools.partial(gather_kernel, n, A, B, S, rank),
        out_shape=jax.ShapeDtypeStruct((rows, width), jnp.bfloat16),
        in_specs=[scalars, scalars, scalars, vmem, any_space, any_space, any_space],
        out_specs=vmem,
        scratch_shapes=[
            pltpu.VMEM((n, 4, quarter_rows, width), weight.dtype),
            pltpu.VMEM((n, pair) + part, bank.dtype),
            pltpu.VMEM(tokens.shape, tokens.dtype),
            pltpu.VMEM((rows, width), jnp.float32),
            pltpu.VMEM((pair, 128 // rank, rows // pair, 128), jnp.float32),
            pltpu.VMEM((n,) + part, bank.dtype),
            pltpu.VMEM((pair,) + part, bank.dtype),
            pltpu.VMEM((pair,) + part, bank.dtype),
            pltpu.VMEM((pair,) + part, bank.dtype),
            dma((7, n, S)),
            dma((4, n, S)),
            dma((4, n, pair)),
            dma((n, pair)),
            dma((n,)),
            dma((n,)),
            dma((2,)),
            dma((4,)),
        ],
        compiler_params=pltpu.CompilerParams(
            collective_id=0, has_side_effects=True, vmem_limit_bytes=44 << 20
        ),
    )(pick, home, length, bias, weight.reshape(4, quarter_rows, width), bank, tokens)


def body(
    tokens,
    value_weight,
    value_bias,
    down_matrices,
    up_matrices,
    adapter_of_block,
    residency,
    block_length,
):
    block_count, block_rows, model_width = tokens.shape
    rank = down_matrices.shape[2]
    out_width = value_weight.shape[1]
    n = lax.axis_size("seq")
    adapter_ids = jnp.arange(residency.shape[0], dtype=jnp.int32)
    bank_slot = jnp.sum(
        jnp.where(adapter_of_block[:, None] == adapter_ids[None, :], residency[None, :], 0), axis=1
    ).astype(jnp.int32)

    fold = 128 // rank
    down_rows = model_width // n // fold
    groups = out_width // 128
    up_rows = rank * groups // n
    pad = -(down_rows + up_rows) % 16
    bank = jnp.concatenate(
        [
            down_matrices[0].reshape(n, fold, down_rows, rank).transpose(0, 2, 1, 3).reshape(n, down_rows, 128),
            up_matrices[0].reshape(n // groups, up_rows, groups, 128).transpose(0, 2, 1, 3).reshape(n, up_rows, 128),
            jnp.zeros((n, pad, 128), down_matrices.dtype),
        ],
        axis=1,
    )
    out = run(
        n,
        tokens.reshape(block_count * block_rows, model_width),
        value_weight,
        value_bias.reshape(1, out_width),
        bank,
        bank_slot % n,
        bank_slot // n,
        block_length,
        block_count,
        rank,
    )
    return out.reshape(block_count, block_rows, out_width)


def solution(mesh):
    in_specs = (
        P(("outer", "rep"), "seq", None),
        P("seq", None),
        P(),
        P(("outer", "rep", "seq"), None, None),
        P(("outer", "rep", "seq"), None, None),
        P("outer"),
        P("outer"),
        P("outer"),
    )
    out_specs = P(("outer", "rep"), "seq", None)
    return jax.shard_map(body, mesh=mesh, in_specs=in_specs, out_specs=out_specs, check_vma=False)
```
